32 devices in a mesh: rows: 8 (over z, x), mp: 4 (over y, core).
Axes of the slice: x: 2, y: 2, z: 4, core: 2. Of those that a mesh axis runs over, the one named last changes fastest.
Arguments:
- hidden: bfloat16 [4096, 1536], P('rows'), may hold values from -6 to 6
- segments: int32 [8, 512], P('rows'), may hold values from 0 to 3, never falling along the last dimension, each value on 1 to 256 neighbouring positions
- granular: int32 [4096], P('rows'), may hold values from 0 to 3, as said below
- norm_gain: bfloat16 [2, 2, 1536], P(None, None, 'rows'), may hold values from 0.5 to 1.5
- norm_bias: bfloat16 [2, 2, 1536], P(None, None, 'rows'), may hold values from -1 to 1
- w_query: bfloat16 [2, 1536, 1536], P(None, 'rows', 'mp'), may hold values from -0.15625 to 0.15625
- w_key: bfloat16 [2, 1536, 1536], P(None, 'rows', 'mp'), may hold values from -0.15625 to 0.15625
- w_value: bfloat16 [2, 1536, 1536], P(None, 'rows', 'mp'), may hold values from -0.15625 to 0.15625
- w_out: bfloat16 [2, 1536, 1536], P(None, 'mp', 'rows'), may hold values from -0.625 to 0.625
- w_up: bfloat16 [2, 1536, 4, 1536], P(None, 'rows', 'mp'), may hold values from -0.15625 to 0.15625
- b_up: bfloat16 [2, 4, 1536], P(None, 'mp', 'rows'), may hold values from -3 to 3
- w_down: bfloat16 [2, 4, 1536, 1536], P(None, 'mp', None, 'rows'), may hold values from -0.15625 to 0.15625
- b_down: bfloat16 [2, 1536], P(None, 'rows'), may hold values from -2 to 2
- cotangent: bfloat16 [4096, 1536], P('rows'), may hold values from -6 to 6
Outputs:
- result: bfloat16 [4096, 1536], P('rows')
- grad_hidden: float32 [4096, 1536], P('rows')
- grad_norm_gain: float32 [2, 2, 1536], P(None, None, 'rows')
- grad_norm_bias: float32 [2, 2, 1536], P(None, None, 'rows')
- grad_query: float32 [2, 1536, 1536], P(None, 'rows', 'mp')
- grad_key: float32 [2, 1536, 1536], P(None, 'rows', 'mp')
- grad_value: float32 [2, 1536, 1536], P(None, 'rows', 'mp')
- grad_out: float32 [2, 1536, 1536], P(None, 'mp', 'rows')
- grad_up: float32 [2, 1536, 4, 1536], P(None, 'rows', 'mp')
- grad_up_bias: float32 [2, 4, 1536], P(None, 'mp', 'rows')
- grad_down: float32 [2, 4, 1536, 1536], P(None, 'mp', None, 'rows')
- grad_down_bias: float32 [2, 1536], P(None, 'rows')
The draws below stay inside these ranges and needn't reach their ends.
Inputs may be any that keep to these rules, and one draw needn't show every extreme that they name: `granular`: in every block of 512 consecutive tokens (a device holds 4096 / rows tokens, so one or more such blocks), at most 256 have any one level; one level, drawn from the seed, has exactly 256 in every such block.
All inputs are finite; a program needn't handle non-finite values.
Results may differ from the reference program's by a relative error of at most 0.03.
Values may be sent and summed in bfloat16 or wider, within the bound.
No kernel may reach another device: no remote copies, remote signals or barrier semaphores. Data moves between devices by JAX's collectives and lax.ppermute only.
A program may use at most 320 MiB of HBM per device.

```python
import math
import jax
import jax.numpy as jnp
import numpy as np
from jax import lax

D = 1536
H = 12
DH = 128
FF = 6144
SEQ_LEN = 512
LAYERS = 2
TOK_DEV = 512
SEQS = 8
TOKENS = 4096
N_MP = 4


def draw_granular(key, part):
    key = jax.random.fold_in(key, 7)
    blocks = TOKENS // TOK_DEV
    capacity = TOK_DEV // 2
    full_level = jax.random.randint(jax.random.fold_in(key, 1), (), 0, 4)
    first_count = jax.random.randint(jax.random.fold_in(key, 2), (blocks,), 0, capacity + 1)
    second_count = jax.random.randint(jax.random.fold_in(key, 3), (blocks,), 0, capacity + 1 - first_count)
    placing = jnp.arange(TOK_DEV)[None, :]
    cut_one = capacity + first_count[:, None]
    cut_two = cut_one + second_count[:, None]
    offset = (placing >= capacity).astype(jnp.int32) + (placing >= cut_one).astype(jnp.int32) + (placing >= cut_two).astype(jnp.int32)
    level_sorted = (full_level + offset) % 4
    order_keys = jax.random.split(jax.random.fold_in(key, 4), blocks)
    orders = jax.vmap(lambda sub_key: jax.random.permutation(sub_key, TOK_DEV))(order_keys)
    levels = jnp.zeros((blocks, TOK_DEV), jnp.int32)
    levels = jax.vmap(lambda level_row, order_row, sorted_row: level_row.at[order_row].set(sorted_row))(levels, orders, level_sorted)
    return levels.reshape(TOKENS).astype(jnp.int32)


def block_levels(stream_key, extent, cuts, least, high):
    def one(dim, blocks):
        draws = jax.random.uniform(jax.random.fold_in(jax.random.fold_in(stream_key, 6), dim), (blocks,), jnp.float32, least / len(cuts), high / len(cuts))
        return jnp.repeat(jnp.exp(draws), extent[dim] // blocks).reshape((-1,) + (1,) * (len(extent) - dim - 1))

    level = one(*cuts[0])
    for cut in cuts[1:]:
        level = level * one(*cut)
    return level


def length_profile(count, total, bound, lean):
    loads = [(1 << 20) // math.isqrt(standing ** lean) + 1 for standing in range(2, count + 1)]
    rest, given = total - bound - (count - 1), [1] * (count - 1)
    while rest > 0:
        free = [i for i in range(count - 1) if given[i] < bound]
        mass, left = sum([loads[i] for i in free]), rest
        for i in free:
            more = min(bound - given[i], max(1, left * loads[i] // mass), rest)
            given[i] = given[i] + more
            rest = rest - more
    return np.array([bound] + given)


def uneven_parts(key, amount, total, reach, skew):
    if amount == 2:
        one = jax.random.randint(key, (), max(1, total - reach), min(reach, total - 1) + 1)
        return jnp.stack([one, total - one])
    sizes = jnp.asarray(length_profile(amount, total, reach, skew), jnp.int32)
    couples = (amount - 1) // 2
    giver, taker = sizes[1:1 + 2 * couples:2], sizes[2:2 + 2 * couples:2]
    room = jnp.minimum(giver - 1, reach - taker)
    shifted = jax.random.randint(jax.random.fold_in(key, 1), (couples,), 0, 1 << 20) % (room + 1)
    sizes = sizes.at[1:1 + 2 * couples:2].set(giver - shifted).at[2:2 + 2 * couples:2].set(taker + shifted)
    return sizes[jax.random.permutation(jax.random.fold_in(key, 2), amount)]


def noise(rng, extent, scale, most, cuts=(), kind=jnp.bfloat16):
    factor_of = block_levels(rng, extent, cuts, -0.22, 0.18) if cuts else 1.0
    values = jax.random.normal(rng, extent, jnp.float32) * scale * factor_of
    return jnp.minimum(jnp.maximum(values, -most), most).astype(kind)


def setup_inputs(seed: int = 0) -> dict:
    streams_of = jax.random.split(jax.random.key(seed), 15)
    hidden = noise(streams_of[0], (TOKENS, D), 1.0, 6.0, ((0, 8),))
    segments = jax.vmap(lambda own: jnp.searchsorted(jnp.cumsum(uneven_parts(own, 4, SEQ_LEN, SEQ_LEN // 2, 1)), jnp.arange(SEQ_LEN), side="right"))(jax.random.split(streams_of[1], SEQS)).reshape((SEQS, SEQ_LEN)).astype(jnp.int32)
    granular = draw_granular(jax.random.fold_in(streams_of[14], 71), 0)
    norm_gain = jnp.clip(1.0 + 0.1 * jax.random.normal(streams_of[3], (LAYERS, 2, D), jnp.float32), 0.5, 1.5).astype(jnp.bfloat16)
    norm_bias = noise(streams_of[4], (LAYERS, 2, D), 0.2, 1.0, ((2, 8),))
    w_query = noise(streams_of[5], (LAYERS, D, H * DH), D ** -0.5, 0.15625, ((1, 8), (2, 4)))
    w_key = noise(streams_of[6], (LAYERS, D, H * DH), D ** -0.5, 0.15625, ((1, 8), (2, 4)))
    w_value = noise(streams_of[7], (LAYERS, D, H * DH), D ** -0.5, 0.15625, ((1, 8), (2, 4)))
    w_out = noise(streams_of[8], (LAYERS, H * DH, D), (H * DH // 16) ** -0.5, 0.625, ((1, 4), (2, 8)))
    w_up = noise(streams_of[9], (LAYERS, D, N_MP, FF // N_MP), D ** -0.5, 0.15625, ((1, 8), (2, 4)))
    b_up = noise(streams_of[10], (LAYERS, N_MP, FF // N_MP), 0.5, 3.0, ((1, 4), (2, 8)))
    w_down = noise(streams_of[11], (LAYERS, N_MP, FF // N_MP, D), (FF // 4) ** -0.5, 0.15625, ((1, 4), (3, 8)))
    b_down = noise(streams_of[12], (LAYERS, D), 0.3, 2.0, ((1, 8),))
    cotangent = noise(streams_of[13], (TOKENS, D), 1.0, 6.0, ((0, 8),))
    return {"hidden": hidden, "segments": segments, "granular": granular, "norm_gain": norm_gain, "norm_bias": norm_bias, "w_query": w_query, "w_key": w_key, "w_value": w_value, "w_out": w_out, "w_up": w_up, "b_up": b_up, "w_down": w_down, "b_down": b_down, "cotangent": cotangent}


@jax.custom_vjp
def low(v):
    return lax.optimization_barrier(v.astype(jnp.bfloat16)).astype(jnp.float32)

@jax.custom_vjp
def low_back(v):
    return v

def low_keep(v):
    return (low(v), None)

def low_pass(kept, grad):
    return (grad,)

def back_keep(v):
    return (v, None)

def back_low(kept, grad):
    return (low(grad),)
low.defvjp(low_keep, low_pass)
low_back.defvjp(back_keep, back_low)
precision_high = lax.Precision.HIGHEST
epsilon = 1e-05
masked_value = -1e+30

def layer_norm(values, norm_scale, offset):
    average = lax.optimization_barrier(jnp.mean(values, axis=-1, keepdims=True))
    centred = values - average
    variance = lax.optimization_barrier(jnp.mean(centred * centred, axis=-1, keepdims=True))
    return centred * lax.rsqrt(variance + epsilon) * norm_scale + offset

def rotary_tables(length, head_width):
    half_width = head_width // 2
    frequency = 10000.0 ** (-jnp.arange(half_width, dtype=jnp.float32) / half_width)
    angles = jnp.arange(length, dtype=jnp.float32)[:, None] * frequency[None, :]
    return (jnp.cos(angles), jnp.sin(angles))

def rotate(values, cosine_table, sine_table):
    half_width = values.shape[-1] // 2
    leading = values[..., :half_width]
    trailing = values[..., half_width:]
    return jnp.concatenate([leading * cosine_table - trailing * sine_table, trailing * cosine_table + leading * sine_table], axis=-1)

def allowed_mask(segment_row):
    position = jnp.arange(segment_row.shape[0])
    return (position[:, None] >= position[None, :]) & (segment_row[:, None] == segment_row[None, :])

def sequence_attention(inputs):
    query_block, key_block, value_block, segment_row = inputs
    scores = jnp.einsum('qhd,khd->hqk', query_block, key_block, precision=precision_high) * DH ** (-0.5)
    scores = low_back(scores)
    scores = jnp.where(allowed_mask(segment_row)[None], scores, masked_value)
    weights = low(jax.nn.softmax(scores, axis=-1))
    return jnp.einsum('hqk,khd->qhd', weights, value_block, precision=precision_high)

def forward(state, segments, granular, norm_gain, norm_bias, w_query, w_key, w_value, w_out, w_up, b_up, w_down, b_down):
    cosine_table, sine_table = rotary_tables(SEQ_LEN, DH)
    cosine_table = cosine_table[:, None, :]
    sine_table = sine_table[:, None, :]
    seq_total = segments.shape[0]
    token_total = state.shape[0]
    full_width = FF // N_MP
    limit = full_width // 8 * jnp.power(2, granular)
    keep = (jnp.arange(full_width)[None, :] < limit[:, None]).astype(jnp.float32)[:, None, :]
    for layer_index in range(LAYERS):
        normed = low(layer_norm(state, norm_gain[layer_index, 0], norm_bias[layer_index, 0]))

        def project(weight):
            projected = jnp.dot(normed, weight[layer_index], precision=precision_high)
            return low_back(projected).reshape(seq_total, SEQ_LEN, H, DH)
        queries = low(rotate(project(w_query), cosine_table, sine_table))
        keyset = low(rotate(project(w_key), cosine_table, sine_table))
        valueset = low(project(w_value))
        mixture = lax.map(jax.checkpoint(sequence_attention), (queries, keyset, valueset, segments))
        mixture = low(low_back(mixture.reshape(token_total, H * DH)))
        state = state + low_back(jnp.dot(mixture, w_out[layer_index], precision=precision_high))
        second = low(low_back(layer_norm(state, norm_gain[layer_index, 1], norm_bias[layer_index, 1])))
        upward = jnp.einsum('td,dmf->tmf', second, w_up[layer_index], precision=precision_high) + b_up[layer_index][None]
        upward = low_back(upward)
        active = low(jax.nn.gelu(upward)) * keep
        downward = jnp.einsum('tmf,mfd->td', active, w_down[layer_index], precision=precision_high) + b_down[layer_index][None]
        state = state + low(low_back(downward))
    return state

def reference(hidden, segments, granular, norm_gain, norm_bias, w_query, w_key, w_value, w_out, w_up, b_up, w_down, b_down, cotangent):
    weights = tuple((weight_arg.astype(jnp.float32) for weight_arg in (norm_gain, norm_bias, w_query, w_key, w_value, w_out, w_up, b_up, w_down, b_down)))

    def wrapped(start_state, *params):
        return forward(start_state, segments, granular, *params)
    output, pullback = jax.vjp(wrapped, hidden.astype(jnp.float32), *weights)
    gradients = pullback(cotangent.astype(jnp.float32))
    return (output.astype(jnp.bfloat16), gradients[0], gradients[1], gradients[2], gradients[3], gradients[4], gradients[5], gradients[6], gradients[7], gradients[8], gradients[9], gradients[10])
```

```python
from functools import partial

import jax
import jax.numpy as jnp
from jax import lax
from jax.experimental import pallas as pl
from jax.experimental.pallas import tpu as pltpu
from jax.sharding import PartitionSpec as P

DH = 128

epsilon = 1e-05
masked_value = -1e30
bf16 = jnp.bfloat16
f32 = jnp.float32


def ring_order(count):
    return list(range(0, count, 2)) + list(range(count - 1, 0, -2))


def whole_blocks(pieces):
    middle = len(pieces) // 2
    return [
        *pieces[:middle],
        jnp.concatenate(pieces[middle : middle + 2], axis=1),
        *pieces[middle + 2 :],
    ]


def tie(*values):
    return lax.optimization_barrier(values)


class Ring:
    def __init__(self, count):
        self.count = count
        self.middle = count // 2
        order = ring_order(count)
        places = [0] * count
        for place, device in enumerate(order):
            places[device] = place
        place = jnp.asarray(places, jnp.int32)[lax.axis_index("rows")]
        self.owners = jnp.asarray(order, jnp.int32)[(place + jnp.arange(count)) % count]
        self.pairs = [(order[i], order[(i + 1) % count]) for i in range(count)]

    def ahead(self, value):
        return lax.ppermute(value, "rows", self.pairs)

    def back(self, value):
        return lax.ppermute(value, "rows", [(b, a) for a, b in self.pairs])


def half_of(extent):
    half = extent // 2
    whole_tiles = (half + 15) // 16 * 16
    return whole_tiles if whole_tiles < extent else half


class Gather:
    handling = 2.2

    def __init__(self, ring, shard):
        self.ring, self.shard = ring, shard
        self.extent = shard.shape[1]
        self.step, self.head, self.tail = 0, [shard], []

    @property
    def done(self):
        return self.step == self.ring.middle

    @property
    def pieces(self):
        return self.head + self.tail

    def start(self, value):
        if self.step == 0:
            value, self.shard = tie(value, self.shard)
            self.head = [self.shard]
            self.forward = self.backward = self.shard
        self.step += 1
        if self.step == self.ring.middle:
            half = half_of(self.extent)
            value, self.forward, self.backward = tie(
                value, self.forward[:, :half], self.backward[:, half:]
            )
        self.size = self.forward.size * 2
        self.flight = self.ring.ahead(self.forward), self.ring.back(self.backward)
        return value

    def finish(self, value):
        value, self.forward, self.backward = tie(value, *self.flight)
        if self.step < self.ring.middle:
            self.head.append(self.backward)
            self.tail.insert(0, self.forward)
        else:
            self.tail = [self.forward, self.backward] + self.tail
        return value


class Scatter:
    handling = 4.5

    def __init__(self, ring, *terms):
        self.ring, self.terms = ring, terms
        self.extent = terms[0].shape[0] // ring.count
        self.step, self.total = 0, None

    @property
    def done(self):
        return self.step == self.ring.middle

    def block(self, place, first=0, last=None):
        last = self.extent if last is None else last
        start = place * self.extent
        return jnp.stack([part[start + first : start + last].astype(f32) for part in self.terms])

    def start(self, value):
        half, count, middle = half_of(self.extent), self.ring.count, self.ring.middle
        if self.step == 0:
            forward = self.block(middle, 0, half)
            backward = self.block(middle, half)
        else:
            forward = self.block(middle - self.step)
            backward = self.block(count - middle + self.step)
            if self.step == 1:
                forward = jnp.concatenate(
                    [forward[:, :half] + self.forward, forward[:, half:]], axis=1
                )
                backward = jnp.concatenate(
                    [backward[:, :half], backward[:, half:] + self.backward], axis=1
                )
            else:
                forward = forward + self.forward
                backward = backward + self.backward
        value, forward, backward = tie(value, forward.astype(bf16), backward.astype(bf16))
        self.step += 1
        self.size = forward.size * 2
        self.flight = self.ring.ahead(forward), self.ring.back(backward)
        return value

    def finish(self, value):
        value, forward, backward = tie(value, *self.flight)
        self.forward, self.backward = forward.astype(f32), backward.astype(f32)
        if self.done:
            self.total = self.block(0) + self.forward + self.backward
        return value


class Belt:
    rate = 0.0214
    lag = 2.0
    patience = 4.0

    def __init__(self, depth):
        self.depth, self.waiting, self.flying = depth, [], []
        self.clock = self.free = 0.0
        self.tight = False

    def add(self, *chains):
        self.waiting.extend(chains)

    def launch(self, value):
        while self.waiting and len(self.flying) < self.depth:
            chain = self.waiting.pop(0)
            value = chain.start(value)
            self.clock += chain.handling
            self.free = max(self.clock, self.free) + chain.size / 1e3 * self.rate
            self.flying.append((self.free + self.lag, chain))
        return value

    def end_first(self, value):
        finish, chain = self.flying.pop(0)
        self.clock = max(self.clock, finish)
        value = chain.finish(value)
        if not chain.done:
            self.waiting.insert(sum(other.step > 0 for other in self.waiting), chain)
        return self.launch(value)

    def catch_up(self, value, until):
        while self.flying and self.flying[0][0] <= until:
            value = self.end_first(value)
        return self.launch(value)

    def busy(self, value, time):
        self.clock += time
        return self.catch_up(value, self.clock + self.patience)

    def idle(self, value, time):
        if self.tight:
            return self.end_first(self.launch(value)) if self.flying or self.waiting else value
        until = self.clock + time
        value = self.catch_up(value, until)
        self.clock = max(self.clock, until)
        return value

    def need(self, value, *chains):
        while any(chain.step == 0 or chain in self.waiting for chain in chains) or any(
            chain is flying for chain in chains for _, flying in self.flying
        ):
            value = self.end_first(self.launch(value))
        return value


class Group:
    def __init__(self, count, belt):
        self.count, self.belt = count, belt
        self.index = lax.axis_index("mp")
        self.bits = [bit for bit in range(count.bit_length() - 1)]

    def side(self, bit):
        return (self.index >> bit) & 1

    def swap(self, value, bit):
        return lax.ppermute(value, "mp", [(i, i ^ (1 << bit)) for i in range(self.count)])

    def own(self, values):
        for bit in self.bits:
            half = values.shape[0] // 2
            values = lax.dynamic_slice_in_dim(values, self.side(bit) * half, half)
        return values

    swap_times = (3.5, 9.5)

    def during(self, value, bit, ticks):
        return self.belt.idle(value, self.swap_times[min(bit, 1)]) if ticks else value

    def scatter(self, terms, ticks=True):
        for bit in self.bits:
            half = terms.shape[0] // 2
            keep = lax.dynamic_slice_in_dim(terms, self.side(bit) * half, half)
            give = lax.dynamic_slice_in_dim(terms, (1 - self.side(bit)) * half, half)
            got = self.swap(give.astype(bf16), bit)
            keep = self.during(keep, bit, ticks)
            terms = keep.astype(f32) + got.astype(f32)
        return terms

    def gather(self, values, ticks=True):
        for bit in reversed(self.bits):
            extent = values.shape[0]
            other = self.swap(values, bit)
            values = self.during(values, bit, ticks)
            whole = jnp.zeros((2 * extent,) + values.shape[1:], values.dtype)
            whole = lax.dynamic_update_slice_in_dim(whole, values, self.side(bit) * extent, 0)
            values = lax.dynamic_update_slice_in_dim(
                whole, other, (1 - self.side(bit)) * extent, 0
            )
        return values

    def total(self, values):
        for bit in self.bits:
            values = values + self.swap(values.astype(bf16), bit).astype(f32)
        return values


def layer_norm(values, gain, shift):
    average = jnp.mean(values, axis=-1, keepdims=True)
    centred = values - average
    variance = jnp.mean(centred * centred, axis=-1, keepdims=True)
    return centred * lax.rsqrt(variance + epsilon) * gain + shift


def layer_norm_pull(values, gain, grad):
    average = jnp.mean(values, axis=-1, keepdims=True)
    centred = values - average
    scale = lax.rsqrt(jnp.mean(centred * centred, axis=-1, keepdims=True) + epsilon)
    unit = centred * scale
    inner = grad * gain
    along = jnp.mean(inner * unit, axis=-1, keepdims=True)
    grad_values = scale * (inner - jnp.mean(inner, axis=-1, keepdims=True) - unit * along)
    return grad_values, jnp.sum(grad * unit, axis=0), jnp.sum(grad, axis=0)


def rotary_tables(length):
    half_width = DH // 2
    frequency = 10000.0 ** (-jnp.arange(half_width, dtype=f32) / half_width)
    angles = jnp.arange(length, dtype=f32)[:, None] * frequency[None, :]
    cosine, sine = jnp.cos(angles), jnp.sin(angles)
    return (
        jnp.concatenate([cosine, cosine], axis=1),
        jnp.concatenate([-sine, sine], axis=1),
    )


def dot(left, right):
    return jnp.dot(left, right, preferred_element_type=f32)


def contract_rows(left, right):
    return lax.dot_general(left, right, (((0,), (0,)), ((), ())), preferred_element_type=f32)


def contract_cols(left, right):
    return lax.dot_general(left, right, (((1,), (1,)), ((), ())), preferred_element_type=f32)


ROWS = 256
short_kernel = pl.CostEstimate(flops=1000, bytes_accessed=1000, transcendentals=0)


def turned(values, cosine, sine):
    return values * cosine + pltpu.roll(values, DH // 2, 1) * sine


def block_probs(query, key, segment_column, segment_row, first):
    scores = contract_cols(query, key) * DH ** (-0.5)
    row = lax.broadcasted_iota(jnp.int32, scores.shape, 0) + first
    column = lax.broadcasted_iota(jnp.int32, scores.shape, 1)
    allowed = (row >= column) & (segment_column == segment_row)
    scores = jnp.where(allowed, scores, masked_value)
    exponent = jnp.exp(scores - jnp.max(scores, axis=-1, keepdims=True))
    return exponent * (1.0 / jnp.sum(exponent, axis=-1, keepdims=True))


def lay_out(pieces, whole, columns=slice(None)):
    start = 0
    for piece in pieces:
        whole[start : start + piece.shape[0], columns] = piece[...]
        start += piece.shape[0]


def pack_kernel(query, key, value, out, pack):
    for first in range(0, query.shape[1], DH):
        for member, source in enumerate((query, key, value, out)):
            place = 4 * first + member * DH
            pack[:, place : place + DH] = source[:, first : first + DH]


def attend_kernel(count, *refs):
    pieces, refs = refs[:count], refs[count:]
    normed, cosine, sine, seg_column, seg_row, *refs = refs
    heads, mixture, terms, normed_t, weight, out_weight, mixtures = refs
    lay_out(pieces, weight)
    step = pl.program_id(0)

    @pl.when(step == 0)
    def _():
        normed_t[...] = normed[...].T

    length = normed.shape[0]
    projected = dot(normed[...], weight[:, : 3 * DH])
    turn = cosine[...], sine[...]
    heads[:, :DH] = turned(projected[:, :DH], *turn).astype(bf16)
    heads[:, DH : 2 * DH] = turned(projected[:, DH : 2 * DH], *turn).astype(bf16)
    heads[:, 2 * DH :] = projected[:, 2 * DH :].astype(bf16)
    for first in range(0, length, ROWS):
        last = first + ROWS
        probs = block_probs(
            heads[first:last, :DH],
            heads[:last, DH : 2 * DH],
            seg_column[first:last, :],
            seg_row[:, :last],
            first,
        )
        mixture[first:last, :] = dot(probs.astype(bf16), heads[:last, 2 * DH :]).astype(bf16)
    place = pl.ds(pl.multiple_of(step * DH, DH), DH)
    out_weight[:, place] = weight[:, 3 * DH :]
    mixtures[:, place] = mixture[...]

    @pl.when(step == pl.num_programs(0) - 1)
    def _():
        terms[...] = contract_cols(mixtures[...], out_weight[...]).astype(bf16)


def attend_pull_kernel(count, *refs):
    pieces, refs = refs[:count], refs[count:]
    grad_attn, normed_t, heads, mixture, cosine, sine, seg_column, seg_row, *refs = refs
    grads, terms, grad_heads, grad_key, grad_value, grad_attn_t, weight, weights, all_grads = refs
    lay_out(pieces, weight)
    step = pl.program_id(0)

    @pl.when(step == 0)
    def _():
        grad_attn_t[...] = grad_attn[...].T

    length = grad_attn.shape[0]
    grad_mixture = dot(grad_attn[...], weight[:, 3 * DH :]).astype(bf16)
    grad_key[...] = jnp.zeros_like(grad_key)
    grad_value[...] = jnp.zeros_like(grad_value)
    scale = DH ** (-0.5)
    for first in range(0, length, ROWS):
        last = first + ROWS
        query = heads[first:last, :DH]
        key = heads[:last, DH : 2 * DH]
        probs = block_probs(query, key, seg_column[first:last, :], seg_row[:, :last], first)
        grad_rows = grad_mixture[first:last]
        grad_probs = contract_cols(grad_rows, heads[:last, 2 * DH :])
        inner = jnp.sum(probs * grad_probs, axis=-1, keepdims=True)
        grad_scores = (probs * (grad_probs - inner)).astype(bf16)
        grad_query = dot(grad_scores, key) * scale
        grad_heads[first:last, :DH] = turned(
            grad_query, cosine[first:last, :], -sine[first:last, :]
        ).astype(bf16)
        grad_key[:last, :] += contract_rows(grad_scores, query)
        grad_value[:last, :] += contract_rows(probs.astype(bf16), grad_rows)
    grad_heads[:, DH : 2 * DH] = turned(
        grad_key[...] * scale, cosine[...], -sine[...]
    ).astype(bf16)
    grad_heads[:, 2 * DH :] = grad_value[...].astype(bf16)
    grads[:, : 3 * DH] = dot(normed_t[...], grad_heads[...]).astype(bf16)
    grads[:, 3 * DH :] = dot(grad_attn_t[...], mixture[...]).astype(bf16)
    place = pl.ds(pl.multiple_of(step * 3 * DH, DH), 3 * DH)
    weights[:, place] = weight[:, : 3 * DH]
    all_grads[:, place] = grad_heads[...]

    @pl.when(step == pl.num_programs(0) - 1)
    def _():
        terms[...] = contract_cols(all_grads[...], weights[...]).astype(bf16)


def fixed(shape):
    return pl.BlockSpec(shape, lambda step: (0, 0))


def first_norm_kernel(values, gain, shift, normed):
    normed[...] = layer_norm(values[...], gain[...], shift[...]).astype(bf16)


def first_norm(values, gain, shift):
    tokens, width = values.shape
    rows = pl.BlockSpec((ROWS, width), lambda step: (step, 0))
    return pl.pallas_call(
        first_norm_kernel,
        grid=(tokens // ROWS,),
        in_specs=[rows, fixed(gain.shape), fixed(shift.shape)],
        out_specs=rows,
        out_shape=jax.ShapeDtypeStruct((tokens, width), bf16),
        cost_estimate=short_kernel,
        name="first_norm",
    )(values, gain, shift)


def by_column(rows, columns):
    return pl.BlockSpec((rows, columns), lambda step: (0, step))


def by_piece(piece, member, columns):
    return pl.BlockSpec((None, piece.shape[1], columns), lambda step: (member, 0, step))


def pack_heads(query, key, value, out, layer):
    share, width = query.shape[1:]
    members = query, key, value, out.transpose(0, 2, 1)
    return pl.pallas_call(
        pack_kernel,
        grid=(1,),
        in_specs=[pl.BlockSpec((None, share, width), lambda step: (layer, 0, 0))] * 4,
        out_specs=pl.BlockSpec((None, share, 4 * width), lambda step: (0, 0, 0)),
        out_shape=jax.ShapeDtypeStruct((1, share, 4 * width), bf16),
        cost_estimate=short_kernel,
        name="pack_heads",
    )(*members)


def attend(normed, pieces, tables):
    tokens, width = normed.shape
    heads = pieces[0].shape[2] // (4 * DH)
    return pl.pallas_call(
        partial(attend_kernel, len(pieces)),
        grid=(heads,),
        in_specs=[
            *[by_piece(piece, 0, 4 * DH) for piece in pieces],
            fixed((tokens, width)),
            *[fixed(table.shape) for table in tables],
        ],
        out_specs=[
            by_column(tokens, 3 * DH),
            by_column(tokens, DH),
            fixed((tokens, width)),
            fixed((width, tokens)),
        ],
        out_shape=[
            jax.ShapeDtypeStruct((tokens, heads * 3 * DH), bf16),
            jax.ShapeDtypeStruct((tokens, heads * DH), bf16),
            jax.ShapeDtypeStruct((tokens, width), bf16),
            jax.ShapeDtypeStruct((width, tokens), bf16),
        ],
        scratch_shapes=[
            pltpu.VMEM((width, 4 * DH), bf16),
            pltpu.VMEM((width, heads * DH), bf16),
            pltpu.VMEM((tokens, heads * DH), bf16),
        ],
        compiler_params=pltpu.CompilerParams(vmem_limit_bytes=40 * 2**20),
        cost_estimate=short_kernel,
        name="attend",
    )(*pieces, normed, *tables)


def attend_pull(grad_attn, normed_t, pieces, heads, mixture, tables):
    tokens, width = grad_attn.shape
    columns = pieces[0].shape[2]
    return pl.pallas_call(
        partial(attend_pull_kernel, len(pieces)),
        grid=(columns // (4 * DH),),
        in_specs=[
            *[by_piece(piece, 0, 4 * DH) for piece in pieces],
            fixed((tokens, width)),
            fixed((width, tokens)),
            by_column(tokens, 3 * DH),
            by_column(tokens, DH),
            *[fixed(table.shape) for table in tables],
        ],
        out_specs=[by_column(width, 4 * DH), fixed((tokens, width))],
        out_shape=[
            jax.ShapeDtypeStruct((width, columns), bf16),
            jax.ShapeDtypeStruct((tokens, width), bf16),
        ],
        scratch_shapes=[
            pltpu.VMEM((tokens, 3 * DH), bf16),
            pltpu.VMEM((tokens, DH), f32),
            pltpu.VMEM((tokens, DH), f32),
            pltpu.VMEM((width, tokens), bf16),
            pltpu.VMEM((width, 4 * DH), bf16),
            pltpu.VMEM((width, columns // 4 * 3), bf16),
            pltpu.VMEM((tokens, columns // 4 * 3), bf16),
        ],
        compiler_params=pltpu.CompilerParams(vmem_limit_bytes=40 * 2**20),
        cost_estimate=short_kernel,
        name="attend_pull",
    )(*pieces, grad_attn, normed_t, heads, mixture, *tables)


def gelu_and_slope(values):
    root = (2.0 / jnp.pi) ** 0.5
    bent = root + (0.044715 * root) * (values * values)
    half = 0.5 + 0.5 * jnp.tanh(values * bent)
    value = values * half
    return value, half + value * (1.0 - half) * (6.0 * bent - 4.0 * root)


UNITS = 512


def add_terms(step, added, total, terms):
    @pl.when(step == 0)
    def _():
        total[...] = added

    @pl.when(step > 0)
    def _():
        total[...] += added

    @pl.when(step == pl.num_programs(0) - 1)
    def _():
        terms[...] = total[...].astype(bf16)


def open_units(second, up, shift, limit, active, slope, second_t):
    @pl.when(pl.program_id(0) == 0)
    def _():
        second_t[...] = second[...].T

    upward = dot(second[...], up[...]) + shift[...]
    value, rise = gelu_and_slope(upward)
    unit = lax.broadcasted_iota(jnp.int32, upward.shape, 1) + pl.program_id(0) * UNITS
    inside = unit < limit[...]
    active[...] = jnp.where(inside, value, 0.0).astype(bf16)
    slope[...] = jnp.where(inside, rise, 0.0).astype(bf16)


def this_cut():
    return pl.ds(pl.multiple_of(pl.program_id(0) * UNITS, UNITS), UNITS)


def units_kernel(count, *refs):
    ups, downs, refs = refs[:count], refs[count : 2 * count], refs[2 * count :]
    second, shift, limit, active, slope, second_t, terms, up, down, all_active = refs
    lay_out(ups, up)
    lay_out(downs, down, this_cut())
    open_units(second, up, shift, limit, active, slope, second_t)
    all_active[:, this_cut()] = active[...]

    @pl.when(pl.program_id(0) == pl.num_programs(0) - 1)
    def _():
        terms[...] = contract_cols(all_active[...], down[...]).astype(bf16)


def last_units_kernel(count, *refs):
    ups, refs = refs[:count], refs[count:]
    second, grad_branch_t, shift, limit, active, slope, second_t, grad_down, up = refs
    lay_out(ups, up)
    open_units(second, up, shift, limit, active, slope, second_t)
    grad_down[...] = dot(grad_branch_t[...], active[...]).astype(bf16)


def units_pull_kernel(count, last, *refs):
    ups, downs, refs = refs[:count], refs[count : 2 * count], refs[2 * count :]
    grad_branch, second_t, slope, active, *refs = refs
    if last:
        grad_up, shift_grad, terms, down, up, all_grads = refs
    else:
        grad_up, grad_down, shift_grad, terms, down, up, all_grads, grad_branch_t = refs
    lay_out(ups, up, this_cut())
    lay_out(downs, down)
    grad_upward = (dot(grad_branch[...], down[...]) * slope[...].astype(f32)).astype(bf16)
    grad_up[...] = dot(second_t[...], grad_upward).astype(bf16)
    shift_grad[...] = jnp.sum(grad_upward.astype(f32), axis=0, keepdims=True)
    all_grads[:, this_cut()] = grad_upward
    if not last:

        @pl.when(pl.program_id(0) == 0)
        def _():
            grad_branch_t[...] = grad_branch[...].T

        grad_down[...] = dot(grad_branch_t[...], active[...]).astype(bf16)

    @pl.when(pl.program_id(0) == pl.num_programs(0) - 1)
    def _():
        terms[...] = contract_cols(all_grads[...], up[...]).astype(bf16)


def units_call(kernel, name, wholes, operands, results, scratch):
    def spec(shape, cut):
        return by_column(shape[0], UNITS) if cut else fixed(shape)

    pieces = [(piece, member) for group, member in wholes for piece in group]
    units = pieces[0][0].shape[2]
    width = sum(piece.shape[1] for piece in wholes[0][0])
    return pl.pallas_call(
        kernel,
        grid=(units // UNITS,),
        in_specs=[
            *[by_piece(piece, member, UNITS) for piece, member in pieces],
            *[spec(part.shape, cut) for part, cut in operands],
        ],
        out_specs=[spec(part.shape, cut) for part, cut in results],
        out_shape=[part for part, _ in results],
        scratch_shapes=[pltpu.VMEM(shape, kind) for shape, kind in scratch],
        compiler_params=pltpu.CompilerParams(vmem_limit_bytes=56 * 2**20),
        cost_estimate=short_kernel,
        name=name,
    )(*[piece for piece, _ in pieces], *[part for part, _ in operands])


def run_units(second, up, down, shift, limit):
    tokens, width = second.shape
    kept = jax.ShapeDtypeStruct((tokens, up[0][0].shape[2]), bf16)
    return units_call(
        partial(units_kernel, len(up[0])),
        "units",
        [up, down],
        [(second, False), (shift, True), (limit, False)],
        [
            (kept, True),
            (kept, True),
            (jax.ShapeDtypeStruct((width, tokens), bf16), False),
            (jax.ShapeDtypeStruct((tokens, width), bf16), False),
        ],
        [((width, UNITS), bf16), ((width, kept.shape[1]), bf16), (kept.shape, bf16)],
    )


def run_last_units(second, up, grad_branch_t, shift, limit):
    tokens, width = second.shape
    units = up[0][0].shape[2]
    kept = jax.ShapeDtypeStruct((tokens, units), bf16)
    return units_call(
        partial(last_units_kernel, len(up[0])),
        "last_units",
        [up],
        [(second, False), (grad_branch_t, False), (shift, True), (limit, False)],
        [
            (kept, True),
            (kept, True),
            (jax.ShapeDtypeStruct((width, tokens), bf16), False),
            (jax.ShapeDtypeStruct((width, units), bf16), True),
        ],
        [((width, UNITS), bf16)],
    )


def branch_kernel(count, *refs):
    downs, (active, terms, total, down) = refs[:count], refs[count:]
    lay_out(downs, down)
    add_terms(pl.program_id(0), contract_cols(active[...], down[...]), total, terms)


def run_branch(active, down):
    tokens, width = active.shape[0], sum(piece.shape[1] for piece in down[0])
    terms = jax.ShapeDtypeStruct((tokens, width), bf16), False
    return units_call(
        partial(branch_kernel, len(down[0])),
        "branch",
        [down],
        [(active, True)],
        [terms],
        [((tokens, width), f32), ((width, UNITS), bf16)],
    )[0]


def run_units_pull(last, grad_branch, second_t, slope, active, up, down):
    tokens, width = grad_branch.shape
    units = up[0][0].shape[2]
    grad = jax.ShapeDtypeStruct((width, units), bf16), True
    shift_grad = jax.ShapeDtypeStruct((1, units), f32), True
    terms = jax.ShapeDtypeStruct((tokens, width), bf16), False
    scratch = [((width, UNITS), bf16), ((width, units), bf16), ((tokens, units), bf16)]
    return units_call(
        partial(units_pull_kernel, len(up[0]), last),
        "units_pull",
        [up, down],
        [(grad_branch, False), (second_t, False), (slope, True), (active, True)],
        [grad, shift_grad, terms] if last else [grad, grad, shift_grad, terms],
        scratch if last else [*scratch, ((width, tokens), bf16)],
    )


def shards(
    hidden,
    segments,
    granular,
    norm_gain,
    norm_bias,
    w_query,
    w_key,
    w_value,
    w_out,
    w_up,
    b_up,
    w_down,
    b_down,
    cotangent,
):
    rows_count = lax.axis_size("rows")
    layers = w_query.shape[0]
    tokens, width = hidden.shape
    seq_count, seq_length = segments.shape
    head_width = w_query.shape[2]
    units = w_up.shape[3]
    share = width // rows_count
    ring = Ring(rows_count)
    belt = Belt(2)
    busy, need = belt.busy, belt.need
    group = Group(lax.axis_size("mp"), belt)

    vector_count = 16
    vectors = Gather(
        ring,
        jnp.concatenate(
            [
                norm_gain.reshape(2 * layers, share),
                norm_bias.reshape(2 * layers, share),
                b_up.reshape(layers, share),
                b_down,
                jnp.zeros((vector_count - 6 * layers, share), bf16),
            ]
        )[None],
    )
    heads_w = [Gather(ring, pack_heads(w_query, w_key, w_value, w_out, 0))]
    belt.add(heads_w[0], vectors)
    (
        hidden,
        cotangent,
        raw_query,
        raw_key,
        raw_value,
        raw_out,
        raw_up,
        raw_down,
    ) = tie(belt.launch(hidden), cotangent, w_query, w_key, w_value, w_out, w_up, w_down)
    belt.flying.reverse()
    features = (ring.owners[:, None] * share + jnp.arange(share)[None, :]).reshape(width)
    turn = (jnp.arange(width)[:, None] == features[None, :]).astype(bf16)
    hidden = dot(hidden, turn)
    position = jnp.arange(seq_count, dtype=segments.dtype)[:, None]
    marks = segments + 4 * position
    tables = tuple(jnp.tile(table, (seq_count, 1)) for table in rotary_tables(seq_length))
    tables += marks.reshape(tokens, 1), marks.reshape(1, tokens)
    limit = (units // 8 * 2**granular)[:, None]
    hidden, limit, *tables = tie(hidden, limit, *tables)

    def pack_units(layer):
        return [raw_up[layer, :, 0], raw_down[layer, 0].T]

    unit_packs = [[jnp.stack(pack_units(layer))] for layer in range(layers - 1)]
    unit_packs.append([part[None] for part in pack_units(layers - 1)])
    head_packs = [
        pack_heads(raw_query, raw_key, raw_value, raw_out, layer) for layer in range(1, layers)
    ]
    raw_cotangent = cotangent
    cotangent = dot(raw_cotangent, turn).astype(bf16)
    cotangent_t = lax.dot_general(
        turn, raw_cotangent, (((0,), (1,)), ((), ())), preferred_element_type=f32
    ).astype(bf16)

    def ring_round(value, *work):
        return tie(belt.end_first(belt.end_first(value)), *work)

    hidden, unit_packs[0][0] = ring_round(hidden, unit_packs[0][0])
    hidden, *head_packs = ring_round(hidden, *head_packs)
    up_w, down_w = [], []
    for layer in range(layers):
        if layer > 0:
            heads_w.append(Gather(ring, head_packs[layer - 1]))
            belt.add(heads_w[layer])
        chains = [Gather(ring, pack) for pack in unit_packs[layer]]
        belt.add(*chains)
        up_w.append((chains[0], 0))
        down_w.append((chains[-1], len(chains) % 2))
    hidden = need(hidden, vectors)
    table = jnp.concatenate([part[0] for part in whole_blocks(vectors.pieces)], axis=1)
    up_shift = contract_cols(table[4 * layers : 5 * layers], turn)
    table = table.astype(f32)
    gains = table[: 2 * layers]
    shifts = table[2 * layers : 4 * layers]
    down_shift = table[5 * layers : 6 * layers]

    state = group.own(hidden)
    normed = first_norm(hidden, gains[:1], shifts[:1])
    def pieces_of(place):
        chain, member = place
        return chain.pieces, member

    kept = []
    for layer in range(layers):
        normed = need(normed, heads_w[layer])
        if layer == 0:
            normed = belt.end_first(normed)
        belt.tight = layer == 0
        heads, mixture, head_terms, normed_t = attend(normed, heads_w[layer].pieces, tables)
        head_terms = busy(head_terms, 10.0)
        middle = state + group.scatter(head_terms)
        belt.clock += 2.5
        second = group.gather(
            layer_norm(middle, gains[2 * layer + 1], shifts[2 * layer + 1]).astype(bf16)
        )
        belt.clock += 2.0
        belt.tight = False
        second = need(second, up_w[layer][0])
        shift = up_shift[layer][None]
        if layer + 1 == layers:
            active, slope, second_t, down_terms = run_last_units(
                second, pieces_of(up_w[layer]), cotangent_t, shift, limit
            )
        else:
            active, slope, second_t, unit_terms = run_units(
                second, pieces_of(up_w[layer]), pieces_of(down_w[layer]), shift, limit
            )
        kept.append((state, normed_t, heads, mixture, middle, second_t, active, slope))
        if layer + 1 < layers:
            unit_terms = busy(unit_terms, 13.0)
            branch = group.scatter(unit_terms) + down_shift[layer]
            belt.clock += 2.5
            state = middle + branch.astype(bf16).astype(f32)
            normed = group.gather(
                layer_norm(state, gains[2 * layer + 2], shifts[2 * layer + 2]).astype(bf16)
            )
            belt.clock += 2.0

    grad_branch = cotangent
    grad_state = group.own(cotangent).astype(f32)
    gain_grads, shift_grads = [None] * (2 * layers), [None] * (2 * layers)
    up_shift_grads, down_shift_grads = [None] * layers, [None] * layers
    heads_g, up_g, down_g = [None] * layers, [None] * layers, [None] * layers
    for layer in reversed(range(layers)):
        layer_input, normed_t, heads, mixture, middle, second_t, active, slope = kept[layer]
        last = layer + 1 == layers
        down_shift_grads[layer] = jnp.sum(grad_branch.astype(f32), axis=0)
        if last:
            active = busy(active, 12.0)
            active = need(active, down_w[layer][0])
        pulled = run_units_pull(
            last,
            grad_branch,
            second_t,
            slope,
            active,
            pieces_of(up_w[layer]),
            pieces_of(down_w[layer]),
        )
        if last:
            up_terms, shift_grad, unit_terms = pulled
            result = middle, active
        else:
            up_terms, down_terms, shift_grad, unit_terms = pulled
        chain = Scatter(ring, up_terms, down_terms)
        up_g[layer], down_g[layer] = (chain, 0), (chain, 1)
        up_shift_grads[layer] = shift_grad[0]
        belt.add(chain)
        unit_terms = busy(unit_terms, 16.0)
        grad_second = group.scatter(unit_terms)
        grad_second = grad_second.astype(bf16).astype(f32)
        pulled, gain_grads[2 * layer + 1], shift_grads[2 * layer + 1] = layer_norm_pull(
            middle, gains[2 * layer + 1], grad_second
        )
        belt.clock += 3.0
        grad_middle = grad_state + pulled
        grad_attn = group.gather(grad_middle.astype(bf16))
        belt.clock += 2.0
        head_terms, grad_terms = attend_pull(
            grad_attn, normed_t, heads_w[layer].pieces, heads, mixture, tables
        )
        if layer > 0:
            heads_g[layer] = Scatter(ring, head_terms)
            belt.add(heads_g[layer])
        grad_terms = busy(grad_terms, 18.0)
        belt.tight = layer == 0
        grad_normed = group.scatter(grad_terms)
        pulled, gain_grads[2 * layer], shift_grads[2 * layer] = layer_norm_pull(
            layer_input, gains[2 * layer], grad_normed
        )
        belt.clock += 3.0
        grad_state = grad_middle + pulled
        if layer > 0:
            grad_branch = group.gather(grad_state.astype(bf16))
            belt.clock += 2.0

    norm_parts = group.total(jnp.stack(gain_grads + shift_grads)).astype(bf16)
    vector_parts = jnp.concatenate(
        [
            norm_parts,
            dot(jnp.stack(up_shift_grads).astype(bf16), turn).astype(bf16),
            jnp.stack(down_shift_grads).astype(bf16),
            jnp.zeros((vector_count - 6 * layers, width), bf16),
        ]
    )
    vector_parts = vector_parts.reshape(vector_count, rows_count, share).transpose(1, 0, 2)
    columns = head_terms.shape[1]
    last_terms = jnp.concatenate(
        [
            head_terms.reshape(rows_count, share, columns),
            jnp.pad(vector_parts, ((0, 0), (0, 0), (0, columns - share))),
        ],
        axis=1,
    ).reshape(-1, columns)
    grad_state, last_terms = tie(grad_state, last_terms)
    heads_g[0] = Scatter(ring, last_terms)
    belt.add(heads_g[0])
    grad_hidden = contract_cols(group.gather(grad_state.astype(bf16)), turn)
    middle, active, grad_hidden = tie(*result, grad_hidden)
    unit_terms = run_branch(active, pieces_of(down_w[-1]))
    state = middle + (group.scatter(unit_terms) + down_shift[-1]).astype(bf16).astype(f32)
    result = contract_cols(group.gather(state.astype(bf16)), turn).astype(bf16)
    chains = [*heads_g, *(chain for chain, _ in up_g + down_g)]
    result = need(result, *chains)
    vector_sums = heads_g[0].total[0, share:, :share]

    def member_grad(chain, member):
        return jnp.concatenate(
            [
                chain.total[0, :share, first + member * DH : first + (member + 1) * DH]
                for first in range(0, 4 * head_width, 4 * DH)
            ],
            axis=1,
        )

    query_grad, key_grad, value_grad, out_grad = (
        [member_grad(chain, member) for chain in heads_g] for member in range(4)
    )
    return (
        result,
        grad_hidden,
        vector_sums[: 2 * layers].reshape(layers, 2, share),
        vector_sums[2 * layers : 4 * layers].reshape(layers, 2, share),
        jnp.stack(query_grad),
        jnp.stack(key_grad),
        jnp.stack(value_grad),
        jnp.stack([part.T for part in out_grad]),
        jnp.stack([chain.total[member] for chain, member in up_g])[:, :, None],
        vector_sums[4 * layers : 5 * layers][:, None],
        jnp.stack([chain.total[member].T for chain, member in down_g])[:, None],
        vector_sums[5 * layers : 6 * layers],
    )


def solution(mesh):
    return jax.shard_map(
        shards,
        mesh=mesh,
        in_specs=(
            P("rows", None),
            P("rows", None),
            P("rows"),
            P(None, None, "rows"),
            P(None, None, "rows"),
            P(None, "rows", "mp"),
            P(None, "rows", "mp"),
            P(None, "rows", "mp"),
            P(None, "mp", "rows"),
            P(None, "rows", "mp", None),
            P(None, "mp", "rows"),
            P(None, "mp", None, "rows"),
            P(None, "rows"),
            P("rows", None),
        ),
        out_specs=(
            P("rows", None),
            P("rows", None),
            P(None, None, "rows"),
            P(None, None, "rows"),
            P(None, "rows", "mp"),
            P(None, "rows", "mp"),
            P(None, "rows", "mp"),
            P(None, "mp", "rows"),
            P(None, "rows", "mp", None),
            P(None, "mp", "rows"),
            P(None, "mp", None, "rows"),
            P(None, "rows"),
        ),
        check_vma=False,
    )
```
